32 devices in a mesh: dp: 8 (over z, y), tp: 4 (over x, core).
Axes of the slice: x: 2, y: 2, z: 4, core: 2. Of those that a mesh axis runs over, the one named last changes fastest.
Arguments:
- query_latent: bfloat16 [3, 128, 128, 512], P(None, 'dp', 'tp'), may hold values from -18 to 18
- query_rotary: bfloat16 [3, 128, 128, 64], P(None, 'dp', 'tp'), may hold values from -18 to 18
- token_latent: bfloat16 [3, 128, 512], P(None, 'dp', 'tp'), may hold values from -5 to 5
- token_rotary: bfloat16 [3, 128, 64], P(None, 'dp', 'tp'), may hold values from -5 to 5
- cache_latent: bfloat16 [96, 8, 128, 512], P('dp'), may hold values from -6 to 6
- cache_rotary: bfloat16 [96, 8, 64, 128], P('dp'), may hold values from -6 to 6
- cache_exponent: int32 [96, 8, 5], P('dp'), may hold values from -1 to 1
- handed_latent: bfloat16 [256, 128, 512], P('dp'), may hold values from -6 to 6
- handed_rotary: bfloat16 [256, 64, 128], P('dp'), may hold values from -6 to 6
- handed_exponent: int32 [256, 5], P('dp'), may hold values from -1 to 1
- block_request: int32 [256], P('dp'), may hold values from -1 to 127, as said below
- block_index: int32 [256], P('dp'), may hold values from -1 to 7, as said below
- lengths: int32 [128], P('dp'), may hold values from 1 to 1024, as said below
- value_up: bfloat16 [128, 512, 128], P('tp'), may hold values from -0.25 to 0.25
Outputs:
- attended: bfloat16 [3, 128, 16384], P(None, 'dp', 'tp')
The draws below stay inside these ranges and needn't reach their ends.
Inputs may be any that keep to these rules, and one draw needn't show every extreme that they name: `lengths`: requests g with g % 16 < 12 have resident cache, the others prefill blocks; some request of the latter kind has the largest length. `block_request`: -1 marks an empty slot; otherwise a request with g % 16 >= 12. Each of its blocks 0 to ceil(lengths[g] / 128) - 1 is in exactly one slot. The 32 slots of one dp index hold at most 4 blocks of the requests of any one owner g // 16; in every draw some owner gets exactly 4 from every dp index. `block_index`: -1 exactly in empty slots.
All inputs are finite; a program needn't handle non-finite values.
Results may differ from the reference program's by a relative error of at most 0.0052.
Values may be sent and summed in bfloat16 or wider, within the bound.
A program may use at most 128 MiB of HBM per device.

```python
import jax
import jax.numpy as jnp
from jax import lax

H = 128
DC = 512
DR = 64
DV = 128
BLK = 128
GROUP = 128
STEPS = 3
NB_MAX = 8
HAND_DEV = 4
RES_DEV = 12
REQUESTS = 128
RESIDENT = 96
CAP = 4
SRC_BLK = 32
HBLOCKS = 256
NGRP = 5
N_DP = 8


def layout(key):
    subkeys = jax.random.split(jax.random.fold_in(key, 17), 7)
    longest = NB_MAX * BLK
    heaviest = jax.random.randint(subkeys[0], (), 0, N_DP)
    drawn = jax.random.randint(subkeys[1], (N_DP, HAND_DEV), 1, longest * 5 // 8 + 1)
    near_full = jax.random.randint(subkeys[2], (HAND_DEV,), longest - BLK + 1, longest + 1)
    full_at = jax.random.randint(subkeys[3], (), 0, HAND_DEV)
    near_full = jnp.where(jnp.arange(HAND_DEV) == full_at, longest, near_full)
    handed = jnp.where((jnp.arange(N_DP) == heaviest)[:, None], near_full[None, :], drawn)
    resident = jax.random.randint(subkeys[4], (N_DP, RES_DEV), 1, longest + 1)
    lengths = jnp.concatenate([resident, handed], axis=1).reshape(-1).astype(jnp.int32)
    counts = (handed + BLK - 1) // BLK
    starts = jnp.cumsum(counts, axis=1) - counts
    totals = jnp.sum(counts, axis=1)
    ordinal = jnp.arange(N_DP * CAP)
    member = jnp.sum((starts[:, None, :] <= ordinal[None, :, None]).astype(jnp.int32), axis=2) - 1
    position = ordinal[None, :] - jnp.take_along_axis(starts, member, axis=1)
    filled = ordinal[None, :] < totals[:, None]
    offsets = jax.random.randint(subkeys[5], (N_DP,), 0, N_DP)
    source = (offsets[:, None] + ordinal[None, :]) % N_DP
    round_number = ordinal[None, :] // N_DP
    shuffles = jax.vmap(lambda single: jax.random.permutation(single, SRC_BLK))(jax.random.split(subkeys[6], N_DP))
    within = shuffles[source, jnp.arange(N_DP)[:, None] * CAP + round_number]
    target = jnp.where(filled, source * SRC_BLK + within, N_DP * SRC_BLK).reshape(-1)
    request = (jnp.arange(N_DP)[:, None] * (RES_DEV + HAND_DEV) + RES_DEV + member).reshape(-1)
    block_request = jnp.full((N_DP * SRC_BLK,), -1, jnp.int32).at[target].set(request.astype(jnp.int32), mode='drop')
    block_index = jnp.full((N_DP * SRC_BLK,), -1, jnp.int32).at[target].set(position.reshape(-1).astype(jnp.int32), mode='drop')
    return (lengths, block_request, block_index)


def draw_lengths(key, part):
    return layout(key)[0]


def draw_block_request(key, part):
    return layout(key)[1]


def draw_block_index(key, part):
    return layout(key)[2]


def draw_query_latent(key, part):
    key = jax.random.fold_in(key, 3)
    return jnp.clip(0.5 * jax.random.normal(key, (STEPS, REQUESTS, H, DC), jnp.float32), -2.5, 2.5).astype(jnp.bfloat16)


def draw_query_rotary(key, part):
    key = jax.random.fold_in(key, 5)
    return jnp.clip(0.5 * jax.random.normal(key, (STEPS, REQUESTS, H, DR), jnp.float32), -2.5, 2.5).astype(jnp.bfloat16)


def draw_token_latent(key, part):
    key = jax.random.fold_in(key, 7)
    return jnp.clip(jax.random.normal(key, (STEPS, REQUESTS, DC), jnp.float32), -5.0, 5.0).astype(jnp.bfloat16)


def draw_token_rotary(key, part):
    key = jax.random.fold_in(key, 11)
    return jnp.clip(jax.random.normal(key, (STEPS, REQUESTS, DR), jnp.float32), -5.0, 5.0).astype(jnp.bfloat16)


def set_ends(entries, rng, low, high):
    dims = entries.shape
    place = [jax.random.randint(jax.random.fold_in(rng, axis), (), 0, dims[axis]) for axis in range(len(dims))]
    entries = entries.at[tuple(place)].set(low)
    longest = dims.index(max(dims))
    place[longest] = (place[longest] + 1) % dims[longest]
    return entries.at[tuple(place)].set(high)


def shard_levels(rng, dims, cuts, smallest, top_value):
    loudness, own = 1.0, jax.random.fold_in(rng, 6)
    for axis_at, shards_of in cuts:
        draws = jnp.exp(jax.random.uniform(jax.random.fold_in(own, axis_at), (shards_of,), jnp.float32, smallest / len(cuts), top_value / len(cuts)))
        loudness = loudness * jnp.repeat(draws, dims[axis_at] // shards_of).reshape([-1 if axis == axis_at else 1 for axis in range(len(dims))])
    return loudness


def bell_draw(key, extent, scale, limit, cuts=(), held_as=jnp.bfloat16):
    entries = jax.random.normal(key, extent, jnp.float32) * scale
    if len(cuts) > 0:
        entries = shard_levels(key, extent, cuts, -0.22, 0.18) * entries
    return jnp.clip(entries, min=-limit, max=limit).astype(held_as)


def setup_inputs(seed: int = 0) -> dict:
    key_list = jax.random.split(jax.random.key(seed), 15)
    return {
        "query_latent": draw_query_latent(jax.random.fold_in(key_list[14], 71), 0),
        "query_rotary": draw_query_rotary(jax.random.fold_in(key_list[14], 71), 0),
        "token_latent": draw_token_latent(jax.random.fold_in(key_list[14], 71), 0),
        "token_rotary": draw_token_rotary(jax.random.fold_in(key_list[14], 71), 0),
        "cache_latent": bell_draw(key_list[4], (RESIDENT, NB_MAX, BLK, DC), 1.0, 6.0, ((0, 8),)),
        "cache_rotary": bell_draw(key_list[5], (RESIDENT, NB_MAX, DR, BLK), 1.0, 6.0, ((0, 8),)),
        "cache_exponent": set_ends(jax.random.randint(key_list[6], (RESIDENT, NB_MAX, NGRP), -1, 2), jax.random.fold_in(key_list[6], 1), -1, 1).astype(jnp.int32),
        "handed_latent": bell_draw(key_list[7], (HBLOCKS, BLK, DC), 1.0, 6.0, ((0, 8),)),
        "handed_rotary": bell_draw(key_list[8], (HBLOCKS, DR, BLK), 1.0, 6.0, ((0, 8),)),
        "handed_exponent": set_ends(jax.random.randint(key_list[9], (HBLOCKS, NGRP), -1, 2), jax.random.fold_in(key_list[9], 1), -1, 1).astype(jnp.int32),
        "block_request": draw_block_request(jax.random.fold_in(key_list[14], 71), 0),
        "block_index": draw_block_index(jax.random.fold_in(key_list[14], 71), 0),
        "lengths": draw_lengths(jax.random.fold_in(key_list[14], 71), 0),
        "value_up": bell_draw(key_list[13], (H, DC, DV), DC ** -0.5, 0.25, ((0, 4),)),
    }


score_scale = 192.0 ** -0.5
masked_score = -1.0e30


def rounded(value):
    return lax.optimization_barrier(value.astype(jnp.bfloat16)).astype(jnp.float32)


def dequantize(latent, rotary, exponent):
    factors = jnp.exp2(exponent.astype(jnp.float32)).astype(latent.dtype)
    columns = jnp.repeat(factors[..., :-1], GROUP, axis=-1)
    return latent * columns[..., None, :], rotary * factors[..., -1:, None]


def reference(query_latent, query_rotary, token_latent, token_rotary, cache_latent, cache_rotary, cache_exponent, handed_latent, handed_rotary, handed_exponent, block_request, block_index, lengths, value_up):
    req_dev = RES_DEV + HAND_DEV
    handed_keys, handed_rot = dequantize(handed_latent, handed_rotary, handed_exponent)
    target_row = jnp.where(block_request >= 0, (block_request // req_dev) * HAND_DEV + block_request % req_dev - RES_DEV, N_DP * HAND_DEV).astype(jnp.int32)
    target_col = jnp.maximum(block_index, 0).astype(jnp.int32)
    placed_latent = jnp.zeros((N_DP * HAND_DEV, NB_MAX, BLK, DC), handed_keys.dtype).at[target_row, target_col].set(handed_keys, mode="drop")
    placed_rotary = jnp.zeros((N_DP * HAND_DEV, NB_MAX, DR, BLK), handed_rot.dtype).at[target_row, target_col].set(handed_rot, mode="drop")
    resident_keys, resident_rot = dequantize(cache_latent, cache_rotary, cache_exponent)
    all_latent = jnp.concatenate([resident_keys.reshape(N_DP, RES_DEV, NB_MAX, BLK, DC), placed_latent.reshape(N_DP, HAND_DEV, NB_MAX, BLK, DC)], axis=1).reshape(N_DP * req_dev, NB_MAX * BLK, DC)
    all_rotary = jnp.concatenate([resident_rot.reshape(N_DP, RES_DEV, NB_MAX, DR, BLK), placed_rotary.reshape(N_DP, HAND_DEV, NB_MAX, DR, BLK)], axis=1).reshape(N_DP * req_dev, NB_MAX, DR, BLK)
    all_rotary = jnp.swapaxes(all_rotary, 2, 3).reshape(N_DP * req_dev, NB_MAX * BLK, DR)
    upward = value_up.astype(jnp.float32)
    offsets = jnp.arange(NB_MAX * BLK)
    step_ids = jnp.arange(STEPS)
    earlier = step_ids[None, :] <= step_ids[:, None]

    def attend(items):
        query_one = items[0].astype(jnp.float32)
        query_rot = items[1].astype(jnp.float32)
        token_one = items[2].astype(jnp.float32)
        token_rot = items[3].astype(jnp.float32)
        keys_one = items[4].astype(jnp.float32)
        keys_rot = items[5].astype(jnp.float32)
        length = items[6]
        scores = (jnp.einsum("shc,kc->shk", query_one, keys_one) + jnp.einsum("shd,kd->shk", query_rot, keys_rot)) * score_scale
        scores = jnp.where((offsets < length)[None, None, :], scores, masked_score)
        fresh = (jnp.einsum("shc,tc->sht", query_one, token_one) + jnp.einsum("shd,td->sht", query_rot, token_rot)) * score_scale
        fresh = jnp.where(earlier[:, None, :], fresh, masked_score)
        peak = jnp.maximum(jnp.max(scores, axis=-1), jnp.max(fresh, axis=-1))
        weights = jnp.exp(scores - peak[..., None])
        fresh_weights = jnp.exp(fresh - peak[..., None])
        total = jnp.sum(weights, axis=-1) + jnp.sum(fresh_weights, axis=-1)
        summed = jnp.einsum("shk,kc->shc", rounded(weights), keys_one) + jnp.einsum("sht,tc->shc", rounded(fresh_weights), token_one)
        mixed = rounded(summed / total[..., None])
        return jnp.einsum("shc,hcv->shv", mixed, upward).astype(jnp.bfloat16).reshape(STEPS, H * DV)

    outputs = lax.map(attend, (jnp.swapaxes(query_latent, 0, 1), jnp.swapaxes(query_rotary, 0, 1), jnp.swapaxes(token_latent, 0, 1), jnp.swapaxes(token_rotary, 0, 1), all_latent, all_rotary, lengths))
    return jnp.swapaxes(outputs, 0, 1)
```

```python
import functools

import jax
import jax.numpy as jnp
from jax import lax
from jax.experimental import pallas as pl
from jax.experimental.pallas import tpu as pltpu
from jax.sharding import PartitionSpec as P

GROUP = 128
FIELDS = 16
LANES = 128
MESH = pl.DeviceIdType.MESH

score_scale = 192.0 ** (-0.5)
masked_score = -1e30
VMEM_LIMIT = 48 * 1024 * 1024


def pack_kernel(req_dev, res_dev, request_ref, index_ref, exponent_ref, latent_ref, rotary_ref,
                send_latent, send_rotary, meta, count, sems):
    owners, rows, _ = send_latent.shape
    rot_rows = send_rotary.shape[1]
    src_blk = request_ref.shape[0]
    cap = src_blk // owners
    per_block = latent_ref.shape[1] // rows
    t = lax.axis_index("tp")

    @pl.loop(0, owners)
    def _(o):
        count[o] = 0
        for k in range(cap):
            meta[o, 0, k * FIELDS] = 0
            meta[o, 0, k * FIELDS + 3] = 0

    @pl.loop(0, src_blk)
    def _(slot):
        request = request_ref[slot]

        @pl.when(request >= 0)
        def _():
            o = lax.div(request, req_dev)
            k = count[o]
            count[o] = k + 1
            base = k * FIELDS
            meta[o, 0, base] = 1
            meta[o, 0, base + 1] = request - o * req_dev - res_dev
            meta[o, 0, base + 2] = index_ref[slot]
            meta[o, 0, base + 3] = slot
            for g in range(exponent_ref.shape[1]):
                meta[o, 0, base + 4 + g] = exponent_ref[slot, g]

    block = lax.div(t, per_block)
    piece = lax.rem(t, per_block)
    copies = []
    for o in range(owners):
        slot = meta[o, 0, block * FIELDS + 3]
        copies.append(pltpu.make_async_copy(
            latent_ref.at[slot, pl.ds(pl.multiple_of(piece * rows, rows), rows)], send_latent.at[o], sems.at[o, 0]))
        copies.append(pltpu.make_async_copy(
            rotary_ref.at[slot, pl.ds(pl.multiple_of(piece * rot_rows, rot_rows), rot_rows)], send_rotary.at[o], sems.at[o, 1]))
    for copy in copies:
        copy.start()
    for copy in copies:
        copy.wait()


def attend(query, rotary_query, keys_ref, rot_blocks, exponent, length):
    blocks = len(rot_blocks)
    block_rows = rot_blocks[0].shape[1]
    width = keys_ref.shape[1]
    group_of = lax.broadcasted_iota(jnp.int32, (1, width), 1) // GROUP
    rot = []
    for j in range(blocks):
        power = jnp.full((1, width), exponent(j, 0), jnp.int32)
        for g in range(1, width // GROUP):
            power = jnp.where(group_of == g, exponent(j, g), power)
        factor = jnp.exp2(power.astype(jnp.float32)).astype(jnp.bfloat16)
        rows = slice(j * block_rows, (j + 1) * block_rows)
        keys_ref[rows, :] = keys_ref[rows, :] * factor
        rot_power = jnp.full((1, block_rows), exponent(j, width // GROUP), jnp.int32)
        rot.append(rot_blocks[j] * jnp.exp2(rot_power.astype(jnp.float32)).astype(jnp.bfloat16))
    keys = keys_ref[...]
    scores = lax.dot_general(query, keys, (((1,), (1,)), ((), ())), preferred_element_type=jnp.float32)
    scores = scores + jnp.dot(rotary_query, jnp.concatenate(rot, axis=1), preferred_element_type=jnp.float32)
    position = lax.broadcasted_iota(jnp.int32, (1, blocks * block_rows), 1)
    scores = jnp.where(position < length, scores * score_scale, masked_score)
    peak = jnp.max(scores, axis=1, keepdims=True)
    weights = jnp.exp(scores - peak)
    total = jnp.sum(weights, axis=1, keepdims=True)
    mix = jnp.dot(weights.astype(jnp.bfloat16), keys, preferred_element_type=jnp.float32)
    return mix, peak, total


def exchange_kernel(owners, heads_groups, query_ref, rotary_ref, lengths_ref, exponent_ref,
                    cache_latent, cache_rotary, send_latent, send_rotary, send_meta, token_latent, token_rotary,
                    got_latent, got_rotary, got_meta, got_token, got_token_rot, mix_ref, stat_ref,
                    keys, rots, key_sems, own_sems, dp_send, dp_recv, x_send, x_recv, core_send, core_recv,
                    tok_send, tok_recv):
    me, t = lax.axis_index("dp"), lax.axis_index("tp")
    across = heads_groups // 2
    partner = t + 1 - 2 * lax.rem(t, 2)
    res_dev, blocks, block_rows, width = cache_latent.shape

    def peer(o):
        return lax.rem(me + o, owners)

    def origin(o):
        return lax.rem(me + owners - o, owners)

    def part_of(k):
        return lax.rem(t + heads_groups - 2 * k, heads_groups)

    barrier = pltpu.get_barrier_semaphore()
    for o in range(1, owners):
        pl.semaphore_signal(barrier, inc=1, device_id=(peer(o), t), device_id_type=MESH)
    for k in range(1, heads_groups):
        pl.semaphore_signal(barrier, inc=1, device_id=(me, lax.rem(t + k, heads_groups)), device_id_type=MESH)
    pl.semaphore_wait(barrier, owners - 1 + heads_groups - 1)

    def dp_copies(o):
        dst = peer(o)
        pairs = ((send_latent.at[dst], got_latent.at[me, t]), (send_rotary.at[dst], got_rotary.at[me, t]),
                 (send_meta.at[dst], got_meta.at[me]))
        return [pltpu.make_async_remote_copy(a, b, dp_send.at[o, n], dp_recv.at[o, n], device_id=(dst, t),
                                             device_id_type=MESH) for n, (a, b) in enumerate(pairs)]

    def dp_arrivals(o):
        src = origin(o)
        pairs = ((got_latent.at[src, t], 0), (got_rotary.at[src, t], 1), (got_meta.at[src], 2))
        return [pltpu.make_async_remote_copy(a, a, dp_send.at[o, n], dp_recv.at[o, n], device_id=(src, t),
                                             device_id_type=MESH) for a, n in pairs]

    def forward(o, part, to, send, recv):
        src = origin(o)
        return [pltpu.make_async_remote_copy(a.at[src, part], a.at[src, part], send.at[n], recv.at[n],
                                             device_id=(me, to), device_id_type=MESH)
                for n, a in enumerate((got_latent, got_rotary))]

    def x_copies(o, k):
        return forward(o, t, lax.rem(t + 2 * k, heads_groups), x_send.at[o, k - 1], x_recv.at[o, k - 1])

    def x_arrivals(o, k):
        return forward(o, part_of(k), part_of(k), x_send.at[o, k - 1], x_recv.at[o, k - 1])

    def core_copies(o, k):
        return forward(o, part_of(k), partner, core_send.at[o, k], core_recv.at[o, k])

    def core_arrivals(o, k):
        part = lax.rem(partner + heads_groups - 2 * k, heads_groups)
        return forward(o, part, partner, core_send.at[o, k], core_recv.at[o, k])

    def token_copies(k):
        to = lax.rem(t + k, heads_groups)
        return [pltpu.make_async_remote_copy(a, b.at[t], tok_send.at[k, n], tok_recv.at[k, n], device_id=(me, to),
                                             device_id_type=MESH)
                for n, (a, b) in enumerate(((token_latent, got_token), (token_rotary, got_token_rot)))]

    def token_arrivals(k):
        src = lax.rem(t + heads_groups - k, heads_groups)
        return [pltpu.make_async_remote_copy(b.at[src], b.at[src], tok_send.at[k, n], tok_recv.at[k, n],
                                             device_id=(me, src), device_id_type=MESH)
                for n, b in enumerate((got_token, got_token_rot))]

    def cache_copies(i, slot):
        return [pltpu.make_async_copy(cache_latent.at[i], keys.at[slot], key_sems.at[slot, 0]),
                pltpu.make_async_copy(cache_rotary.at[i], rots.at[slot], key_sems.at[slot, 1])]

    for copy in cache_copies(0, 0):
        copy.start()
    for o in range(1, owners):
        for copy in dp_copies(o):
            copy.start()
    own = [pltpu.make_async_copy(send_meta.at[me], got_meta.at[me], own_sems.at[0]),
           pltpu.make_async_copy(token_latent, got_token.at[t], own_sems.at[1]),
           pltpu.make_async_copy(token_rotary, got_token_rot.at[t], own_sems.at[2])]
    for copy in own:
        copy.start()
    for k in range(1, heads_groups):
        for copy in token_copies(k):
            copy.start()

    def first_hop(o):
        for copy in dp_arrivals(o):
            copy.wait_recv()
        for k in range(1, across):
            for copy in x_copies(o, k):
                copy.start()
        for copy in core_copies(o, 0):
            copy.start()

    def second_hop(o):
        for k in range(1, across):
            for copy in x_arrivals(o, k):
                copy.wait_recv()
            for copy in core_copies(o, k):
                copy.start()

    first_at = {}
    second_at = {}
    for o in range(1, owners):
        first_at.setdefault(min(res_dev - 1, 2 + (o * 7) // (owners - 1)), []).append(o)
        second_at.setdefault(min(res_dev - 1, 4 + (o * 7) // (owners - 1)), []).append(o)

    @pl.loop(0, res_dev)
    def _(i):
        slot = lax.rem(i, 2)

        @pl.when(i + 1 < res_dev)
        def _():
            for copy in cache_copies(i + 1, 1 - slot):
                copy.start()

        for copy in cache_copies(i, slot):
            copy.wait()
        steps, _, heads, _ = query_ref.shape
        rows = steps * heads
        query = query_ref[:, i].reshape(rows, width)
        rotary_query = rotary_ref[:, i].reshape(rows, rotary_ref.shape[3])
        key_view = keys.at[slot].reshape(blocks * block_rows, width)
        mix, peak, total = attend(query, rotary_query, key_view, [rots[slot, j] for j in range(blocks)],
                                  lambda j, g: exponent_ref[i, j, g], lengths_ref[i])
        mix_ref[i] = mix
        lane = lax.broadcasted_iota(jnp.int32, (rows, LANES), 1)
        stat_ref[i] = jnp.where(lane == 0, peak, total)
        for at, hops in first_at.items():
            @pl.when(i == at)
            def _(hops=hops):
                for o in hops:
                    first_hop(o)
        for at, hops in second_at.items():
            @pl.when(i == at)
            def _(hops=hops):
                for o in hops:
                    second_hop(o)

    for copy in own:
        copy.wait()
    for k in range(1, heads_groups):
        for copy in token_arrivals(k):
            copy.wait_recv()
        for copy in token_copies(k):
            copy.wait_send()
    for o in range(1, owners):
        for copy in dp_copies(o):
            copy.wait_send()
        for k in range(1, across):
            for copy in x_copies(o, k):
                copy.wait_send()
        for k in range(across):
            for copy in core_copies(o, k):
                copy.wait_send()
            for copy in core_arrivals(o, k):
                copy.wait_recv()


def finish_kernel(query_ref, rotary_ref, lengths_ref, meta, mix_ref, stat_ref, token_ref, token_rot_ref,
                  handed_latent, handed_rotary, got_latent, got_rotary, mixed_ref, keys, rots, powers, sems):
    me = lax.axis_index("dp")
    hand, key_rows, width = keys.shape
    owners, groups, rows, _ = got_latent.shape
    rot_rows = got_rotary.shape[2]
    block_rows = handed_latent.shape[1]
    blocks = key_rows // block_rows
    per_block = block_rows // rows
    cap = groups // per_block
    steps, req_dev, heads, _ = query_ref.shape
    res_dev = req_dev - hand
    groups_of_exponents = width // GROUP + 1

    keys[...] = jnp.zeros_like(keys)
    rots[...] = jnp.zeros_like(rots)

    @pl.loop(0, hand * blocks)
    def _(n):
        for g in range(groups_of_exponents):
            powers[n * 8 + g] = 0

    def each_copy(act):
        @pl.loop(0, owners)
        def _(d):
            for k in range(cap):
                base = k * FIELDS

                @pl.when(meta[d, 0, base] == 1)
                def _(k=k, base=base):
                    i, b, slot = meta[d, 0, base + 1], meta[d, 0, base + 2], meta[d, 0, base + 3]
                    for g in range(groups_of_exponents):
                        powers[(i * blocks + b) * 8 + g] = meta[d, 0, base + 4 + g]
                    for p in range(per_block):
                        at = pl.multiple_of(b * block_rows + p * rows, rows)
                        to_keys = keys.at[i, pl.ds(at, rows)]
                        to_rots = rots.at[i * blocks + b, pl.ds(p * rot_rows, rot_rows)]

                        @pl.when(d == me)
                        def _():
                            act(pltpu.make_async_copy(handed_latent.at[slot, pl.ds(p * rows, rows)], to_keys,
                                                      sems.at[d, k * per_block + p, 0]))
                            act(pltpu.make_async_copy(handed_rotary.at[slot, pl.ds(p * rot_rows, rot_rows)], to_rots,
                                                      sems.at[d, k * per_block + p, 1]))

                        @pl.when(d != me)
                        def _():
                            act(pltpu.make_async_copy(got_latent.at[d, k * per_block + p], to_keys,
                                                      sems.at[d, k * per_block + p, 0]))
                            act(pltpu.make_async_copy(got_rotary.at[d, k * per_block + p], to_rots,
                                                      sems.at[d, k * per_block + p, 1]))

    each_copy(lambda copy: copy.start())

    def add_tokens(r, query, rotary_query, mix, peak, total):
        tokens, token_rot = token_ref[r], token_rot_ref[r]
        nt = (((1,), (1,)), ((), ()))
        fresh = (lax.dot_general(query, tokens, nt, preferred_element_type=jnp.float32)
                 + lax.dot_general(rotary_query, token_rot, nt, preferred_element_type=jnp.float32)) * score_scale
        step = lax.broadcasted_iota(jnp.int32, fresh.shape, 0) // heads
        fresh = jnp.where(lax.broadcasted_iota(jnp.int32, fresh.shape, 1) <= step, fresh, masked_score)
        top = jnp.maximum(peak, jnp.max(fresh, axis=1, keepdims=True))
        fresh = jnp.exp(fresh - top)
        shrink = jnp.exp(peak - top)
        total = total * shrink + jnp.sum(fresh, axis=1, keepdims=True)
        mix = mix * shrink + jnp.dot(fresh.astype(jnp.bfloat16), tokens, preferred_element_type=jnp.float32)
        mixed_ref[:, r] = (mix / total).astype(jnp.bfloat16).reshape(steps, heads, width)

    def queries(r):
        return (query_ref[:, r].reshape(steps * heads, width),
                rotary_ref[:, r].reshape(steps * heads, rotary_ref.shape[3]))

    @pl.loop(0, res_dev)
    def _(r):
        query, rotary_query = queries(r)
        add_tokens(r, query, rotary_query, mix_ref[r], stat_ref[r][:, 0:1], stat_ref[r][:, 1:2])

    each_copy(lambda copy: copy.wait())

    @pl.loop(0, hand)
    def _(i):
        query, rotary_query = queries(res_dev + i)
        mix, peak, total = attend(query, rotary_query, keys.at[i], [rots[i * blocks + j] for j in range(blocks)],
                                  lambda j, g: powers[(i * blocks + j) * 8 + g], lengths_ref[res_dev + i])
        add_tokens(res_dev + i, query, rotary_query, mix, peak, total)


def local(
    query_latent,
    query_rotary,
    token_latent,
    token_rotary,
    cache_latent,
    cache_rotary,
    cache_exponent,
    handed_latent,
    handed_rotary,
    handed_exponent,
    block_request,
    block_index,
    lengths,
    value_up,
):
    owners, groups = lax.axis_size("dp"), lax.axis_size("tp")
    req_dev = lengths.shape[0]
    res_dev, blocks, block_rows, width = cache_latent.shape
    rot_width = cache_rotary.shape[2]
    hand = req_dev - res_dev
    src_blk = block_request.shape[0]
    cap = src_blk // owners
    steps, _, heads, _ = query_latent.shape
    rows, rot_rows = cap * block_rows // groups, cap * rot_width // groups
    across = groups // 2
    bf16, f32 = jnp.bfloat16, jnp.float32
    shape = jax.ShapeDtypeStruct
    hbm, vmem, smem = (pl.BlockSpec(memory_space=m) for m in (pl.ANY, pltpu.VMEM, pltpu.SMEM))
    dma = pltpu.SemaphoreType.DMA

    send_latent, send_rotary, send_meta = pl.pallas_call(
        functools.partial(pack_kernel, req_dev, res_dev),
        out_shape=[shape((owners, rows, width), bf16), shape((owners, rot_rows, block_rows), bf16),
                   shape((owners, 1, LANES), jnp.int32)],
        in_specs=[smem, smem, smem, hbm, hbm],
        out_specs=[hbm, hbm, smem],
        scratch_shapes=[pltpu.SMEM((owners,), jnp.int32), dma((owners, 2))],
        name="pack",
    )(block_request, block_index, handed_exponent, handed_latent, handed_rotary)

    got_latent, got_rotary, got_meta, got_token, got_token_rot, mix, stat = pl.pallas_call(
        functools.partial(exchange_kernel, owners, groups),
        out_shape=[shape((owners, groups, rows, width), bf16), shape((owners, groups, rot_rows, block_rows), bf16),
                   shape((owners, 1, LANES), jnp.int32), shape((groups,) + token_latent.shape, bf16),
                   shape((groups,) + token_rotary.shape, bf16), shape((res_dev, steps * heads, width), f32),
                   shape((res_dev, steps * heads, LANES), f32)],
        in_specs=[vmem, vmem, smem, smem] + [hbm] * 7,
        out_specs=[hbm] * 5 + [vmem, vmem],
        scratch_shapes=[pltpu.VMEM((2, blocks, block_rows, width), bf16),
                        pltpu.VMEM((2, blocks, rot_width, block_rows), bf16),
                        dma((2, 2)), dma((3,)), dma((owners, 3)), dma((owners, 3)),
                        dma((owners, across - 1, 2)), dma((owners, across - 1, 2)),
                        dma((owners, across, 2)), dma((owners, across, 2)),
                        dma((groups, 2)), dma((groups, 2))],
        compiler_params=pltpu.CompilerParams(collective_id=0, has_side_effects=True, vmem_limit_bytes=VMEM_LIMIT),
        name="exchange",
    )(query_latent, query_rotary, lengths, cache_exponent, cache_latent, cache_rotary, send_latent, send_rotary,
      send_meta, token_latent, token_rotary)

    def by_request(got):
        whole = jnp.transpose(got, (2, 1, 0, 3)).reshape(req_dev, steps, -1)
        return jnp.pad(whole, ((0, 0), (0, 16 - steps), (0, 0)))

    mixed = pl.pallas_call(
        finish_kernel,
        out_shape=shape((steps, req_dev, heads, width), bf16),
        in_specs=[vmem, vmem, smem, smem, vmem, vmem, vmem, vmem, hbm, hbm, hbm, hbm],
        out_specs=vmem,
        scratch_shapes=[pltpu.VMEM((hand, blocks * block_rows, width), bf16),
                        pltpu.VMEM((hand * blocks, rot_width, block_rows), bf16),
                        pltpu.SMEM((hand * blocks * 8,), jnp.int32), dma((owners, groups, 2))],
        compiler_params=pltpu.CompilerParams(vmem_limit_bytes=VMEM_LIMIT),
        name="finish",
    )(query_latent, query_rotary, lengths, got_meta, mix, stat, by_request(got_token), by_request(got_token_rot),
      handed_latent, handed_rotary, got_latent, got_rotary)

    output = jnp.einsum("srhc,hcv->srhv", mixed, value_up, preferred_element_type=f32).astype(bf16)
    return output.reshape(steps, req_dev, -1)


def solution(mesh):
    placed = (
        P(None, "dp", "tp", None),
        P(None, "dp", "tp", None),
        P(None, "dp", "tp"),
        P(None, "dp", "tp"),
        P("dp", None, None, None),
        P("dp", None, None, None),
        P("dp", None, None),
        P("dp", None, None),
        P("dp", None, None),
        P("dp", None),
        P("dp"),
        P("dp"),
        P("dp"),
        P("tp", None, None),
    )
    return jax.shard_map(
        local, mesh=mesh, in_specs=placed, out_specs=P(None, "dp", "tp"), check_vma=False
    )
```

```python
import functools

import jax
import jax.numpy as jnp
from jax import lax
from jax.experimental import pallas as pl
from jax.experimental.pallas import tpu as pltpu
from jax.sharding import PartitionSpec as P

GROUP = 128
FIELDS = 16
LANES = 128
MESH = pl.DeviceIdType.MESH

score_scale = 192.0 ** (-0.5)
masked_score = -1e30
VMEM_LIMIT = 48 * 1024 * 1024


def scaled(latent, rotary, exponents):
    factors = [jnp.broadcast_to(jnp.exp2(exponents[:, g:g + 1].astype(jnp.float32)).astype(jnp.bfloat16), (1, GROUP))
               for g in range(exponents.shape[1])]
    return latent * jnp.concatenate(factors[:-1], axis=1), rotary * factors[-1][:, :1]


def pack_kernel(req_dev, res_dev, request_ref, index_ref, exponent_ref, latent_ref, rotary_ref,
                send_latent, send_rotary, own_latent, own_rotary, meta, count, sems, own_sems):
    owners, rows, _ = send_latent.shape
    rot_rows = send_rotary.shape[1]
    src_blk = request_ref.shape[0]
    cap = src_blk // owners
    per_block = latent_ref.shape[1] // rows
    me, t = lax.axis_index("dp"), lax.axis_index("tp")

    @pl.loop(0, owners)
    def _(o):
        count[o] = 0
        for k in range(cap):
            for n in range(4):
                meta[o, 0, k * FIELDS + n] = 0

    @pl.loop(0, src_blk)
    def _(slot):
        request = request_ref[slot]

        @pl.when(request >= 0)
        def _():
            o = lax.div(request, req_dev)
            k = count[o]
            count[o] = k + 1
            base = k * FIELDS
            meta[o, 0, base] = 1
            meta[o, 0, base + 1] = request - o * req_dev - res_dev
            meta[o, 0, base + 2] = index_ref[slot]
            meta[o, 0, base + 3] = slot

    block = lax.div(t, per_block)
    piece = lax.rem(t, per_block)

    def send_copies(o):
        slot = meta[o, 0, block * FIELDS + 3]
        return [pltpu.make_async_copy(latent_ref.at[slot, pl.ds(pl.multiple_of(piece * rows, rows), rows)],
                                      send_latent.at[o], sems.at[o, 0]),
                pltpu.make_async_copy(
                    rotary_ref.at[slot, pl.ds(pl.multiple_of(piece * rot_rows, rot_rows), rot_rows)],
                    send_rotary.at[o], sems.at[o, 1])]

    def own_copies(k):
        slot = meta[me, 0, k * FIELDS + 3]
        return [pltpu.make_async_copy(latent_ref.at[slot], own_latent.at[k], own_sems.at[k, 0]),
                pltpu.make_async_copy(rotary_ref.at[slot], own_rotary.at[k], own_sems.at[k, 1])]

    for o in range(owners):
        for copy in send_copies(o):
            copy.start()
    for k in range(cap):
        for copy in own_copies(k):
            copy.start()
    for o in range(owners):
        for copy in send_copies(o):
            copy.wait()
        exponents = exponent_ref[pl.ds(meta[o, 0, block * FIELDS + 3], 1), :]
        send_latent[o], send_rotary[o] = scaled(send_latent[o], send_rotary[o], exponents)
    for k in range(cap):
        for copy in own_copies(k):
            copy.wait()
        exponents = exponent_ref[pl.ds(meta[me, 0, k * FIELDS + 3], 1), :]
        own_latent[k], own_rotary[k] = scaled(own_latent[k], own_rotary[k], exponents)


def attend(request, query, rotary_query, keys, rot, tokens, token_rot, length, req_dev, heads):
    nt = (((1,), (1,)), ((), ()))
    scores = lax.dot_general(query, keys, nt, preferred_element_type=jnp.float32)
    scores = (scores + jnp.dot(rotary_query, rot, preferred_element_type=jnp.float32)) * score_scale
    position = lax.broadcasted_iota(jnp.int32, (1, keys.shape[0]), 1)
    scores = jnp.where(position < length, scores, masked_score)
    fresh = (lax.dot_general(query, tokens, nt, preferred_element_type=jnp.float32)
             + lax.dot_general(rotary_query, token_rot, nt, preferred_element_type=jnp.float32)) * score_scale
    step = lax.broadcasted_iota(jnp.int32, fresh.shape, 0) // heads
    column = lax.broadcasted_iota(jnp.int32, fresh.shape, 1)
    fresh = jnp.where((lax.rem(column, req_dev) == request) & (column // req_dev <= step), fresh, masked_score)
    peak = jnp.maximum(jnp.max(scores, axis=1, keepdims=True), jnp.max(fresh, axis=1, keepdims=True))
    weights = jnp.exp(scores - peak)
    fresh = jnp.exp(fresh - peak)
    total = jnp.sum(weights, axis=1, keepdims=True) + jnp.sum(fresh, axis=1, keepdims=True)
    mix = (jnp.dot(weights.astype(jnp.bfloat16), keys, preferred_element_type=jnp.float32)
           + jnp.dot(fresh.astype(jnp.bfloat16), tokens, preferred_element_type=jnp.float32))
    return (mix / total).astype(jnp.bfloat16)


def exchange_kernel(owners, heads_groups, lengths_ref, exponent_ref, query_ref, rotary_ref,
                    cache_latent, cache_rotary, send_latent, send_rotary, send_meta, token_latent, token_rotary,
                    got_latent, got_rotary, got_meta, tokens, token_rot, mixed_ref,
                    keys, rots, queries, rot_queries, mixes, got_token, got_token_rot,
                    key_sems, mix_sems, own_sems, dp_send, dp_recv, x_send, x_recv, core_send, core_recv,
                    tok_send, tok_recv):
    me, t = lax.axis_index("dp"), lax.axis_index("tp")
    across = heads_groups // 2
    partner = t + 1 - 2 * lax.rem(t, 2)
    res_dev, blocks, block_rows, width = cache_latent.shape

    def peer(o):
        return lax.rem(me + o, owners)

    def origin(o):
        return lax.rem(me + owners - o, owners)

    def part_of(k):
        return lax.rem(t + heads_groups - 2 * k, heads_groups)

    barrier = pltpu.get_barrier_semaphore()
    for o in range(1, owners):
        pl.semaphore_signal(barrier, inc=1, device_id=(peer(o), t), device_id_type=MESH)
    for k in range(1, heads_groups):
        pl.semaphore_signal(barrier, inc=1, device_id=(me, lax.rem(t + k, heads_groups)), device_id_type=MESH)
    pl.semaphore_wait(barrier, owners - 1 + heads_groups - 1)

    def dp_copies(o):
        dst = peer(o)
        pairs = ((send_latent.at[dst], got_latent.at[me, t]), (send_rotary.at[dst], got_rotary.at[me, t]),
                 (send_meta.at[dst], got_meta.at[me]))
        return [pltpu.make_async_remote_copy(a, b, dp_send.at[o, n], dp_recv.at[o, n], device_id=(dst, t),
                                             device_id_type=MESH) for n, (a, b) in enumerate(pairs)]

    def dp_arrivals(o):
        src = origin(o)
        pairs = ((got_latent.at[src, t], 0), (got_rotary.at[src, t], 1), (got_meta.at[src], 2))
        return [pltpu.make_async_remote_copy(a, a, dp_send.at[o, n], dp_recv.at[o, n], device_id=(src, t),
                                             device_id_type=MESH) for a, n in pairs]

    def forward(o, part, to, send, recv):
        src = origin(o)
        return [pltpu.make_async_remote_copy(a.at[src, part], a.at[src, part], send.at[n], recv.at[n],
                                             device_id=(me, to), device_id_type=MESH)
                for n, a in enumerate((got_latent, got_rotary))]

    def x_copies(o, k):
        return forward(o, t, lax.rem(t + 2 * k, heads_groups), x_send.at[o, k - 1], x_recv.at[o, k - 1])

    def x_arrivals(o, k):
        return forward(o, part_of(k), part_of(k), x_send.at[o, k - 1], x_recv.at[o, k - 1])

    def core_copies(o, k):
        return forward(o, part_of(k), partner, core_send.at[o, k], core_recv.at[o, k])

    def core_arrivals(o, k):
        part = lax.rem(partner + heads_groups - 2 * k, heads_groups)
        return forward(o, part, partner, core_send.at[o, k], core_recv.at[o, k])

    def token_copies(k):
        to = lax.rem(t + k, heads_groups)
        return [pltpu.make_async_remote_copy(a, b.at[t], tok_send.at[k, n], tok_recv.at[k, n], device_id=(me, to),
                                             device_id_type=MESH)
                for n, (a, b) in enumerate(((token_latent, got_token), (token_rotary, got_token_rot)))]

    def token_arrivals(k):
        src = lax.rem(t + heads_groups - k, heads_groups)
        return [pltpu.make_async_remote_copy(b.at[src], b.at[src], tok_send.at[k, n], tok_recv.at[k, n],
                                             device_id=(me, src), device_id_type=MESH)
                for n, b in enumerate((got_token, got_token_rot))]

    def cache_copies(i, slot):
        return [pltpu.make_async_copy(cache_latent.at[i], keys.at[slot], key_sems.at[slot, 0]),
                pltpu.make_async_copy(cache_rotary.at[i], rots.at[slot], key_sems.at[slot, 1]),
                pltpu.make_async_copy(query_ref.at[:, i], queries.at[slot], key_sems.at[slot, 2]),
                pltpu.make_async_copy(rotary_ref.at[:, i], rot_queries.at[slot], key_sems.at[slot, 3])]

    def mix_copy(i, slot):
        return pltpu.make_async_copy(mixes.at[slot], mixed_ref.at[:, i], mix_sems.at[slot])

    for copy in cache_copies(0, 0):
        copy.start()
    for k in range(1, heads_groups):
        for copy in token_copies(k):
            copy.start()
    for o in range(1, owners):
        for copy in dp_copies(o):
            copy.start()
    own = [pltpu.make_async_copy(send_meta.at[me], got_meta.at[me], own_sems.at[0]),
           pltpu.make_async_copy(token_latent, got_token.at[t], own_sems.at[1]),
           pltpu.make_async_copy(token_rotary, got_token_rot.at[t], own_sems.at[2])]
    for copy in own:
        copy.start()
    for copy in own:
        copy.wait()
    for k in range(1, heads_groups):
        for copy in token_arrivals(k):
            copy.wait_recv()
    steps, req_dev = got_token.shape[1:3]
    heads = query_ref.shape[2]
    for part in range(heads_groups):
        piece, rot_piece = got_token.shape[3], got_token_rot.shape[3]
        tokens[:, part * piece:(part + 1) * piece] = got_token[part].reshape(steps * req_dev, piece)
    token_rot[...] = jnp.concatenate(
        [got_token_rot[part].reshape(steps * req_dev, got_token_rot.shape[3]) for part in range(heads_groups)], axis=1)

    def first_hop(o):
        for copy in dp_arrivals(o):
            copy.wait_recv()
        for k in range(1, across):
            for copy in x_copies(o, k):
                copy.start()
        for copy in core_copies(o, 0):
            copy.start()

    def second_hop(o):
        for k in range(1, across):
            for copy in x_arrivals(o, k):
                copy.wait_recv()
            for copy in core_copies(o, k):
                copy.start()

    first_at = {}
    second_at = {}
    for o in range(1, owners):
        first_at.setdefault(min(res_dev - 1, 2 + (o * 7) // (owners - 1)), []).append(o)
        second_at.setdefault(min(res_dev - 1, 4 + (o * 7) // (owners - 1)), []).append(o)

    @pl.loop(0, res_dev)
    def _(i):
        slot = lax.rem(i, 2)

        @pl.when(i + 1 < res_dev)
        def _():
            for copy in cache_copies(i + 1, 1 - slot):
                copy.start()

        for copy in cache_copies(i, slot):
            copy.wait()
        @pl.when(i >= 2)
        def _():
            mix_copy(i - 2, slot).wait()

        rot = []
        for j in range(blocks):
            keys[slot, j], block_rot = scaled(keys[slot, j], rots[slot, j], exponent_ref[i, pl.ds(j, 1), :])
            rot.append(block_rot)
        mixed = attend(i, queries[slot].reshape(steps * heads, width),
                       rot_queries[slot].reshape(steps * heads, rot_queries.shape[3]),
                       keys[slot].reshape(blocks * block_rows, width), jnp.concatenate(rot, axis=1),
                       tokens[...], token_rot[...], lengths_ref[i], req_dev, heads)
        mixes[slot] = mixed.reshape(steps, heads, width)
        mix_copy(i, slot).start()
        for at, hops in first_at.items():
            @pl.when(i == at)
            def _(hops=hops):
                for o in hops:
                    first_hop(o)
        for at, hops in second_at.items():
            @pl.when(i == at)
            def _(hops=hops):
                for o in hops:
                    second_hop(o)

    for i in range(max(res_dev - 2, 0), res_dev):
        mix_copy(i, i % 2).wait()
    for k in range(1, heads_groups):
        for copy in token_copies(k):
            copy.wait_send()
    for o in range(1, owners):
        for copy in dp_copies(o):
            copy.wait_send()
        for k in range(1, across):
            for copy in x_copies(o, k):
                copy.wait_send()
        for k in range(across):
            for copy in core_copies(o, k):
                copy.wait_send()
            for copy in core_arrivals(o, k):
                copy.wait_recv()


def finish_kernel(lengths_ref, meta, tokens, token_rot, query_ref, rotary_ref, own_latent, own_rotary,
                  got_latent, got_rotary, partly_mixed, mixed_ref, keys, rots, queries, rot_queries, mixes, sems, query_sems,
                  mix_sems):
    me = lax.axis_index("dp")
    hand, blocks, block_rows, width = keys.shape
    owners, groups, rows, _ = got_latent.shape
    rot_rows = got_rotary.shape[2]
    per_block = block_rows // rows
    cap = groups // per_block
    steps, req_dev, heads, _ = query_ref.shape
    res_dev = req_dev - hand

    def query_copies(i):
        return [pltpu.make_async_copy(query_ref.at[:, res_dev + i], queries.at[i], query_sems.at[i, 0]),
                pltpu.make_async_copy(rotary_ref.at[:, res_dev + i], rot_queries.at[i], query_sems.at[i, 1])]

    for i in range(hand):
        for copy in query_copies(i):
            copy.start()
    keys[...] = jnp.zeros_like(keys)
    rots[...] = jnp.zeros_like(rots)

    def each_copy(act):
        @pl.loop(0, owners)
        def _(d):
            for k in range(cap):
                base = k * FIELDS

                @pl.when(meta[d, 0, base] == 1)
                def _(k=k, base=base):
                    i, b = meta[d, 0, base + 1], meta[d, 0, base + 2]
                    for p in range(per_block):
                        part = k * per_block + p
                        to_keys = keys.at[i, b, pl.ds(p * rows, rows)]
                        to_rots = rots.at[i, b, pl.ds(p * rot_rows, rot_rows)]

                        @pl.when(d == me)
                        def _():
                            act(pltpu.make_async_copy(own_latent.at[k, pl.ds(p * rows, rows)], to_keys,
                                                      sems.at[d, part, 0]))
                            act(pltpu.make_async_copy(own_rotary.at[k, pl.ds(p * rot_rows, rot_rows)], to_rots,
                                                      sems.at[d, part, 1]))

                        @pl.when(d != me)
                        def _():
                            act(pltpu.make_async_copy(got_latent.at[d, part], to_keys, sems.at[d, part, 0]))
                            act(pltpu.make_async_copy(got_rotary.at[d, part], to_rots, sems.at[d, part, 1]))

    each_copy(lambda copy: copy.start())
    for i in range(hand):
        for copy in query_copies(i):
            copy.wait()
    each_copy(lambda copy: copy.wait())

    def mix_copy(i):
        return pltpu.make_async_copy(mixes.at[i], mixed_ref.at[:, res_dev + i], mix_sems.at[i])

    @pl.loop(0, hand)
    def _(i):
        mixed = attend(res_dev + i, queries[i].reshape(steps * heads, width),
                       rot_queries[i].reshape(steps * heads, rot_queries.shape[3]),
                       keys[i].reshape(blocks * block_rows, width),
                       jnp.concatenate([rots[i, j] for j in range(blocks)], axis=1),
                       tokens[...], token_rot[...], lengths_ref[res_dev + i], req_dev, heads)
        mixes[i] = mixed.reshape(steps, heads, width)
        mix_copy(i).start()

    for i in range(hand):
        mix_copy(i).wait()


def local(
    query_latent,
    query_rotary,
    token_latent,
    token_rotary,
    cache_latent,
    cache_rotary,
    cache_exponent,
    handed_latent,
    handed_rotary,
    handed_exponent,
    block_request,
    block_index,
    lengths,
    value_up,
):
    owners, groups = lax.axis_size("dp"), lax.axis_size("tp")
    req_dev = lengths.shape[0]
    res_dev, blocks, block_rows, width = cache_latent.shape
    rot_width = cache_rotary.shape[2]
    hand = req_dev - res_dev
    src_blk = block_request.shape[0]
    cap = src_blk // owners
    steps, _, heads, _ = query_latent.shape
    rows, rot_rows = cap * block_rows // groups, cap * rot_width // groups
    across = groups // 2
    bf16, f32 = jnp.bfloat16, jnp.float32
    shape = jax.ShapeDtypeStruct
    hbm, vmem, smem = (pl.BlockSpec(memory_space=m) for m in (pl.ANY, pltpu.VMEM, pltpu.SMEM))
    dma = pltpu.SemaphoreType.DMA

    send_latent, send_rotary, own_latent, own_rotary, send_meta = pl.pallas_call(
        functools.partial(pack_kernel, req_dev, res_dev),
        out_shape=[shape((owners, rows, width), bf16), shape((owners, rot_rows, block_rows), bf16),
                   shape((cap, block_rows, width), bf16), shape((cap, rot_width, block_rows), bf16),
                   shape((owners, 1, LANES), jnp.int32)],
        in_specs=[smem, smem, vmem, hbm, hbm],
        out_specs=[vmem, vmem, vmem, vmem, smem],
        scratch_shapes=[pltpu.SMEM((owners,), jnp.int32), dma((owners, 2)), dma((cap, 2))],
        compiler_params=pltpu.CompilerParams(vmem_limit_bytes=VMEM_LIMIT),
        name="pack",
    )(block_request, block_index, handed_exponent, handed_latent, handed_rotary)

    got_latent, got_rotary, got_meta, tokens, token_rot, mixed = pl.pallas_call(
        functools.partial(exchange_kernel, owners, groups),
        out_shape=[shape((owners, groups, rows, width), bf16), shape((owners, groups, rot_rows, block_rows), bf16),
                   shape((owners, 1, LANES), jnp.int32), shape((steps * req_dev, width), bf16),
                   shape((steps * req_dev, query_rotary.shape[3]), bf16), shape((steps, req_dev, heads, width), bf16)],
        in_specs=[smem, vmem] + [hbm] * 9,
        out_specs=[vmem, vmem, vmem, vmem, vmem, hbm],
        scratch_shapes=[pltpu.VMEM((2, blocks, block_rows, width), bf16),
                        pltpu.VMEM((2, blocks, rot_width, block_rows), bf16),
                        pltpu.VMEM((2, steps, heads, width), bf16),
                        pltpu.VMEM((2, steps, heads, query_rotary.shape[3]), bf16),
                        pltpu.VMEM((2, steps, heads, width), bf16),
                        pltpu.VMEM((groups,) + token_latent.shape, bf16),
                        pltpu.VMEM((groups,) + token_rotary.shape, bf16),
                        dma((2, 4)), dma((2,)), dma((3,)), dma((owners, 3)), dma((owners, 3)),
                        dma((owners, across - 1, 2)), dma((owners, across - 1, 2)),
                        dma((owners, across, 2)), dma((owners, across, 2)),
                        dma((groups, 2)), dma((groups, 2))],
        compiler_params=pltpu.CompilerParams(collective_id=0, has_side_effects=True, vmem_limit_bytes=VMEM_LIMIT),
        name="exchange",
    )(lengths, cache_exponent, query_latent, query_rotary, cache_latent, cache_rotary, send_latent, send_rotary,
      send_meta, token_latent, token_rotary)

    mixed = pl.pallas_call(
        finish_kernel,
        out_shape=shape((steps, req_dev, heads, width), bf16),
        in_specs=[smem, smem, vmem, vmem] + [hbm] * 7,
        out_specs=hbm,
        input_output_aliases={10: 0},
        scratch_shapes=[pltpu.VMEM((hand, blocks, block_rows, width), bf16),
                        pltpu.VMEM((hand, blocks, rot_width, block_rows), bf16),
                        pltpu.VMEM((hand, steps, heads, width), bf16),
                        pltpu.VMEM((hand, steps, heads, query_rotary.shape[3]), bf16),
                        pltpu.VMEM((hand, steps, heads, width), bf16),
                        dma((owners, groups, 2)), dma((hand, 2)), dma((hand,))],
        compiler_params=pltpu.CompilerParams(vmem_limit_bytes=VMEM_LIMIT),
        name="finish",
    )(lengths, got_meta, tokens, token_rot, query_latent, query_rotary, own_latent, own_rotary, got_latent, got_rotary,
      mixed)

    output = jnp.einsum("srhc,hcv->srhv", mixed, value_up, preferred_element_type=f32).astype(bf16)
    return output.reshape(steps, req_dev, -1)


def solution(mesh):
    placed = (
        P(None, "dp", "tp", None),
        P(None, "dp", "tp", None),
        P(None, "dp", "tp"),
        P(None, "dp", "tp"),
        P("dp", None, None, None),
        P("dp", None, None, None),
        P("dp", None, None),
        P("dp", None, None),
        P("dp", None, None),
        P("dp", None),
        P("dp"),
        P("dp"),
        P("dp"),
        P("tp", None, None),
    )
    return jax.shard_map(
        local, mesh=mesh, in_specs=placed, out_specs=P(None, "dp", "tp"), check_vma=False
    )
```

```python
import functools

import jax
import jax.numpy as jnp
from jax import lax
from jax.experimental import pallas as pl
from jax.experimental.pallas import tpu as pltpu
from jax.sharding import PartitionSpec as P

GROUP = 128
FIELDS = 16
LANES = 128
MESH = pl.DeviceIdType.MESH

PIECES = 4
ROUNDS_AHEAD = 2
FIRST_EVENT = 3
EVENT_STEP = 3
RING = 4


def FLOW_ORDER(owners):
    low = owners // RING
    order = []
    for side in range(low):
        for turn, ring in enumerate((2, 1, 3, 0)):
            order.append(ring * low + (side + turn) % low)
    return [o for o in order if o > 0]


score_scale = 192.0 ** (-0.5)
masked_score = -1e30
VMEM_LIMIT = 48 * 1024 * 1024


def scaled(latent, rotary, exponents):
    factors = [jnp.broadcast_to(jnp.exp2(exponents[:, g:g + 1].astype(jnp.float32)).astype(jnp.bfloat16), (1, GROUP))
               for g in range(exponents.shape[1])]
    return latent * jnp.concatenate(factors[:-1], axis=1), rotary * factors[-1][:, :1]


def pack_kernel(req_dev, res_dev, request_ref, index_ref, exponent_ref, latent_ref, rotary_ref,
                send_latent, send_rotary, own_latent, own_rotary, meta, count, sems, own_sems):
    owners, rows, _ = send_latent.shape
    rot_rows = send_rotary.shape[1]
    src_blk = request_ref.shape[0]
    cap = src_blk // owners
    per_block = latent_ref.shape[1] // rows
    me, t = lax.axis_index("dp"), lax.axis_index("tp")

    @pl.loop(0, owners)
    def _(o):
        count[o] = 0
        for k in range(cap):
            for n in range(4):
                meta[o, 0, k * FIELDS + n] = 0

    @pl.loop(0, src_blk)
    def _(slot):
        request = request_ref[slot]

        @pl.when(request >= 0)
        def _():
            o = lax.div(request, req_dev)
            k = count[o]
            count[o] = k + 1
            base = k * FIELDS
            meta[o, 0, base] = 1
            meta[o, 0, base + 1] = request - o * req_dev - res_dev
            meta[o, 0, base + 2] = index_ref[slot]
            meta[o, 0, base + 3] = slot

    block = lax.div(t, per_block)
    piece = lax.rem(t, per_block)

    def send_copies(o):
        slot = meta[o, 0, block * FIELDS + 3]
        return [pltpu.make_async_copy(latent_ref.at[slot, pl.ds(pl.multiple_of(piece * rows, rows), rows)],
                                      send_latent.at[o], sems.at[o, 0]),
                pltpu.make_async_copy(
                    rotary_ref.at[slot, pl.ds(pl.multiple_of(piece * rot_rows, rot_rows), rot_rows)],
                    send_rotary.at[o], sems.at[o, 1])]

    def own_copies(k):
        slot = meta[me, 0, k * FIELDS + 3]
        return [pltpu.make_async_copy(latent_ref.at[slot], own_latent.at[k], own_sems.at[k, 0]),
                pltpu.make_async_copy(rotary_ref.at[slot], own_rotary.at[k], own_sems.at[k, 1])]

    for o in range(owners):
        for copy in send_copies(o):
            copy.start()
    for k in range(cap):
        for copy in own_copies(k):
            copy.start()
    for o in range(owners):
        for copy in send_copies(o):
            copy.wait()
        exponents = exponent_ref[pl.ds(meta[o, 0, block * FIELDS + 3], 1), :]
        send_latent[o], send_rotary[o] = scaled(send_latent[o], send_rotary[o], exponents)
    for k in range(cap):
        for copy in own_copies(k):
            copy.wait()
        exponents = exponent_ref[pl.ds(meta[me, 0, k * FIELDS + 3], 1), :]
        own_latent[k], own_rotary[k] = scaled(own_latent[k], own_rotary[k], exponents)


def attend(request, query, rotary_query, keys, rot, tokens, token_rot, length, req_dev, heads):
    nt = (((1,), (1,)), ((), ()))
    scores = lax.dot_general(query, keys, nt, preferred_element_type=jnp.float32)
    scores = (scores + jnp.dot(rotary_query, rot, preferred_element_type=jnp.float32)) * score_scale
    position = lax.broadcasted_iota(jnp.int32, (1, keys.shape[0]), 1)
    scores = jnp.where(position < length, scores, masked_score)
    fresh = (lax.dot_general(query, tokens, nt, preferred_element_type=jnp.float32)
             + lax.dot_general(rotary_query, token_rot, nt, preferred_element_type=jnp.float32)) * score_scale
    step = lax.broadcasted_iota(jnp.int32, fresh.shape, 0) // heads
    column = lax.broadcasted_iota(jnp.int32, fresh.shape, 1)
    fresh = jnp.where((lax.rem(column, req_dev) == request) & (column // req_dev <= step), fresh, masked_score)
    peak = jnp.maximum(jnp.max(scores, axis=1, keepdims=True), jnp.max(fresh, axis=1, keepdims=True))
    weights = jnp.exp(scores - peak)
    fresh = jnp.exp(fresh - peak)
    total = jnp.sum(weights, axis=1, keepdims=True) + jnp.sum(fresh, axis=1, keepdims=True)
    mix = (jnp.dot(weights.astype(jnp.bfloat16), keys, preferred_element_type=jnp.float32)
           + jnp.dot(fresh.astype(jnp.bfloat16), tokens, preferred_element_type=jnp.float32))
    return (mix / total).astype(jnp.bfloat16)


def exchange_kernel(owners, heads_groups, lengths_ref, exponent_ref, query_ref, rotary_ref,
                    cache_latent, cache_rotary, send_latent, send_rotary, send_meta, token_latent, token_rotary,
                    got_latent, got_rotary, got_meta, tokens, token_rot, mixed_ref,
                    keys, rots, queries, rot_queries, mixes, got_token, got_token_rot,
                    key_sems, mix_sems, own_sems, dp_send, dp_recv, x_send, x_recv, core_send, core_recv,
                    tok_send, tok_recv):
    me, t = lax.axis_index("dp"), lax.axis_index("tp")
    across = heads_groups // 2
    partner = t + 1 - 2 * lax.rem(t, 2)
    res_dev, blocks, block_rows, width = cache_latent.shape

    low = owners // RING

    def shifted(o, sign):
        ring, side = o // low, o % low
        return lax.rem(lax.div(me, low) + RING + sign * ring, RING) * low + lax.rem(me + low + sign * side, low)

    def peer(o):
        return shifted(o, 1)

    def origin(o):
        return shifted(o, -1)

    def part_of(k):
        return lax.rem(t + heads_groups - 2 * k, heads_groups)

    barrier = pltpu.get_barrier_semaphore()
    for o in range(1, owners):
        pl.semaphore_signal(barrier, inc=1, device_id=(peer(o), t), device_id_type=MESH)
    for k in range(1, heads_groups):
        pl.semaphore_signal(barrier, inc=1, device_id=(me, lax.rem(t + k, heads_groups)), device_id_type=MESH)
    pl.semaphore_wait(barrier, owners - 1 + heads_groups - 1)

    rows = send_latent.shape[1]
    pieces = min(PIECES, rows // 16)
    step_rows = rows // pieces

    def dp_copies(o, p):
        dst = peer(o)
        cut = pl.ds(p * step_rows, step_rows)
        pairs = [(send_latent.at[dst, cut], got_latent.at[me, t, cut], p)]
        if p == 0:
            pairs += [(send_rotary.at[dst], got_rotary.at[me, t], pieces), (send_meta.at[dst], got_meta.at[me], pieces + 1)]
        return [pltpu.make_async_remote_copy(a, b, dp_send.at[o, n], dp_recv.at[o, n], device_id=(dst, t),
                                             device_id_type=MESH) for a, b, n in pairs]

    def dp_arrivals(o, p):
        src = origin(o)
        landed = [(got_latent.at[src, t, pl.ds(p * step_rows, step_rows)], p)]
        if p == 0:
            landed += [(got_rotary.at[src, t], pieces), (got_meta.at[src], pieces + 1)]
        return [pltpu.make_async_remote_copy(a, a, dp_send.at[o, n], dp_recv.at[o, n], device_id=(src, t),
                                             device_id_type=MESH) for a, n in landed]

    def forward(o, part, to, send, recv):
        src = origin(o)
        return [pltpu.make_async_remote_copy(a.at[src, part], a.at[src, part], send.at[n], recv.at[n],
                                             device_id=(me, to), device_id_type=MESH)
                for n, a in enumerate((got_latent, got_rotary))]

    def x_forward(o, k, p, part, to):
        src = origin(o)
        moved = [(got_latent.at[src, part, pl.ds(p * step_rows, step_rows)], p)]
        if p == 0:
            moved.append((got_rotary.at[src, part], pieces))
        return [pltpu.make_async_remote_copy(a, a, x_send.at[o, k - 1, n], x_recv.at[o, k - 1, n], device_id=(me, to),
                                             device_id_type=MESH) for a, n in moved]

    def x_copies(o, k, p):
        return x_forward(o, k, p, t, lax.rem(t + 2 * k, heads_groups))

    def x_arrivals(o, k, p):
        return x_forward(o, k, p, part_of(k), part_of(k))

    def core_copies(o, k):
        return forward(o, part_of(k), partner, core_send.at[o, k], core_recv.at[o, k])

    def core_arrivals(o, k):
        part = lax.rem(partner + heads_groups - 2 * k, heads_groups)
        return forward(o, part, partner, core_send.at[o, k], core_recv.at[o, k])

    def token_copies(k):
        to = lax.rem(t + k, heads_groups)
        return [pltpu.make_async_remote_copy(a, b.at[t], tok_send.at[k, n], tok_recv.at[k, n], device_id=(me, to),
                                             device_id_type=MESH)
                for n, (a, b) in enumerate(((token_latent, got_token), (token_rotary, got_token_rot)))]

    def token_arrivals(k):
        src = lax.rem(t + heads_groups - k, heads_groups)
        return [pltpu.make_async_remote_copy(b.at[src], b.at[src], tok_send.at[k, n], tok_recv.at[k, n],
                                             device_id=(me, src), device_id_type=MESH)
                for n, b in enumerate((got_token, got_token_rot))]

    def cache_copies(i, slot):
        return [pltpu.make_async_copy(cache_latent.at[i], keys.at[slot], key_sems.at[slot, 0]),
                pltpu.make_async_copy(cache_rotary.at[i], rots.at[slot], key_sems.at[slot, 1]),
                pltpu.make_async_copy(query_ref.at[:, i], queries.at[slot], key_sems.at[slot, 2]),
                pltpu.make_async_copy(rotary_ref.at[:, i], rot_queries.at[slot], key_sems.at[slot, 3])]

    def mix_copy(i, slot):
        return pltpu.make_async_copy(mixes.at[slot], mixed_ref.at[:, i], mix_sems.at[slot])

    for copy in cache_copies(0, 0):
        copy.start()
    for k in range(1, heads_groups):
        for copy in token_copies(k):
            copy.start()
    order = FLOW_ORDER(owners)
    for p in range(min(ROUNDS_AHEAD, pieces)):
        for o in order:
            for copy in dp_copies(o, p):
                copy.start()
    own = [pltpu.make_async_copy(send_meta.at[me], got_meta.at[me], own_sems.at[0]),
           pltpu.make_async_copy(token_latent, got_token.at[t], own_sems.at[1]),
           pltpu.make_async_copy(token_rotary, got_token_rot.at[t], own_sems.at[2])]
    for copy in own:
        copy.start()
    for copy in own:
        copy.wait()
    for k in range(1, heads_groups):
        for copy in token_arrivals(k):
            copy.wait_recv()
    steps, req_dev = got_token.shape[1:3]
    heads = query_ref.shape[2]
    for part in range(heads_groups):
        piece, rot_piece = got_token.shape[3], got_token_rot.shape[3]
        tokens[:, part * piece:(part + 1) * piece] = got_token[part].reshape(steps * req_dev, piece)
    token_rot[...] = jnp.concatenate(
        [got_token_rot[part].reshape(steps * req_dev, got_token_rot.shape[3]) for part in range(heads_groups)], axis=1)

    def arrive(p):
        for o in order:
            for copy in dp_arrivals(o, p):
                copy.wait_recv()
            for k in range(1, across):
                for copy in x_copies(o, k, p):
                    copy.start()
            for copy in dp_copies(o, p):
                copy.wait_send()
            if p + ROUNDS_AHEAD < pieces:
                for copy in dp_copies(o, p + ROUNDS_AHEAD):
                    copy.start()
            if p == pieces - 1:
                for copy in core_copies(o, 0):
                    copy.start()

    events = {}
    for p in range(pieces):
        events.setdefault(min(FIRST_EVENT + p * EVENT_STEP, res_dev), []).append(p)

    @pl.loop(0, res_dev)
    def _(i):
        slot = lax.rem(i, 2)

        @pl.when(i + 1 < res_dev)
        def _():
            for copy in cache_copies(i + 1, 1 - slot):
                copy.start()

        for copy in cache_copies(i, slot):
            copy.wait()
        @pl.when(i >= 2)
        def _():
            mix_copy(i - 2, slot).wait()

        rot = []
        for j in range(blocks):
            keys[slot, j], block_rot = scaled(keys[slot, j], rots[slot, j], exponent_ref[i, pl.ds(j, 1), :])
            rot.append(block_rot)
        mixed = attend(i, queries[slot].reshape(steps * heads, width),
                       rot_queries[slot].reshape(steps * heads, rot_queries.shape[3]),
                       keys[slot].reshape(blocks * block_rows, width), jnp.concatenate(rot, axis=1),
                       tokens[...], token_rot[...], lengths_ref[i], req_dev, heads)
        mixes[slot] = mixed.reshape(steps, heads, width)
        mix_copy(i, slot).start()
        for at, due in events.items():
            if at < res_dev:
                @pl.when(i == at)
                def _(due=due):
                    for p in due:
                        arrive(p)

    for p in events.get(res_dev, []):
        arrive(p)
    for o in order:
        for k in range(1, across):
            for p in range(pieces):
                for copy in x_arrivals(o, k, p):
                    copy.wait_recv()
            for copy in core_copies(o, k):
                copy.start()
    for i in range(max(res_dev - 2, 0), res_dev):
        mix_copy(i, i % 2).wait()
    for k in range(1, heads_groups):
        for copy in token_copies(k):
            copy.wait_send()
    for o in range(1, owners):
        for k in range(1, across):
            for p in range(pieces):
                for copy in x_copies(o, k, p):
                    copy.wait_send()
        for k in range(across):
            for copy in core_copies(o, k):
                copy.wait_send()
            for copy in core_arrivals(o, k):
                copy.wait_recv()


def finish_kernel(lengths_ref, meta, tokens, token_rot, query_ref, rotary_ref, own_latent, own_rotary,
                  got_latent, got_rotary, partly_mixed, mixed_ref, keys, rots, queries, rot_queries, mixes, sems, query_sems,
                  mix_sems):
    me = lax.axis_index("dp")
    hand, blocks, block_rows, width = keys.shape
    owners, groups, rows, _ = got_latent.shape
    rot_rows = got_rotary.shape[2]
    per_block = block_rows // rows
    cap = groups // per_block
    steps, req_dev, heads, _ = query_ref.shape
    res_dev = req_dev - hand

    def query_copies(i):
        return [pltpu.make_async_copy(query_ref.at[:, res_dev + i], queries.at[i], query_sems.at[i, 0]),
                pltpu.make_async_copy(rotary_ref.at[:, res_dev + i], rot_queries.at[i], query_sems.at[i, 1])]

    for i in range(hand):
        for copy in query_copies(i):
            copy.start()
    keys[...] = jnp.zeros_like(keys)
    rots[...] = jnp.zeros_like(rots)

    def each_copy(act):
        @pl.loop(0, owners)
        def _(d):
            for k in range(cap):
                base = k * FIELDS

                @pl.when(meta[d, 0, base] == 1)
                def _(k=k, base=base):
                    i, b = meta[d, 0, base + 1], meta[d, 0, base + 2]
                    for p in range(per_block):
                        part = k * per_block + p
                        to_keys = keys.at[i, b, pl.ds(p * rows, rows)]
                        to_rots = rots.at[i, b, pl.ds(p * rot_rows, rot_rows)]

                        @pl.when(d == me)
                        def _():
                            act(pltpu.make_async_copy(own_latent.at[k, pl.ds(p * rows, rows)], to_keys,
                                                      sems.at[d, part, 0]))
                            act(pltpu.make_async_copy(own_rotary.at[k, pl.ds(p * rot_rows, rot_rows)], to_rots,
                                                      sems.at[d, part, 1]))

                        @pl.when(d != me)
                        def _():
                            act(pltpu.make_async_copy(got_latent.at[d, part], to_keys, sems.at[d, part, 0]))
                            act(pltpu.make_async_copy(got_rotary.at[d, part], to_rots, sems.at[d, part, 1]))

    each_copy(lambda copy: copy.start())
    for i in range(hand):
        for copy in query_copies(i):
            copy.wait()
    each_copy(lambda copy: copy.wait())

    def mix_copy(i):
        return pltpu.make_async_copy(mixes.at[i], mixed_ref.at[:, res_dev + i], mix_sems.at[i])

    @pl.loop(0, hand)
    def _(i):
        mixed = attend(res_dev + i, queries[i].reshape(steps * heads, width),
                       rot_queries[i].reshape(steps * heads, rot_queries.shape[3]),
                       keys[i].reshape(blocks * block_rows, width),
                       jnp.concatenate([rots[i, j] for j in range(blocks)], axis=1),
                       tokens[...], token_rot[...], lengths_ref[res_dev + i], req_dev, heads)
        mixes[i] = mixed.reshape(steps, heads, width)
        mix_copy(i).start()

    for i in range(hand):
        mix_copy(i).wait()


def local(
    query_latent,
    query_rotary,
    token_latent,
    token_rotary,
    cache_latent,
    cache_rotary,
    cache_exponent,
    handed_latent,
    handed_rotary,
    handed_exponent,
    block_request,
    block_index,
    lengths,
    value_up,
):
    owners, groups = lax.axis_size("dp"), lax.axis_size("tp")
    req_dev = lengths.shape[0]
    res_dev, blocks, block_rows, width = cache_latent.shape
    rot_width = cache_rotary.shape[2]
    hand = req_dev - res_dev
    src_blk = block_request.shape[0]
    cap = src_blk // owners
    steps, _, heads, _ = query_latent.shape
    rows, rot_rows = cap * block_rows // groups, cap * rot_width // groups
    across = groups // 2
    bf16, f32 = jnp.bfloat16, jnp.float32
    shape = jax.ShapeDtypeStruct
    hbm, vmem, smem = (pl.BlockSpec(memory_space=m) for m in (pl.ANY, pltpu.VMEM, pltpu.SMEM))
    dma = pltpu.SemaphoreType.DMA

    send_latent, send_rotary, own_latent, own_rotary, send_meta = pl.pallas_call(
        functools.partial(pack_kernel, req_dev, res_dev),
        out_shape=[shape((owners, rows, width), bf16), shape((owners, rot_rows, block_rows), bf16),
                   shape((cap, block_rows, width), bf16), shape((cap, rot_width, block_rows), bf16),
                   shape((owners, 1, LANES), jnp.int32)],
        in_specs=[smem, smem, vmem, hbm, hbm],
        out_specs=[vmem, vmem, vmem, vmem, smem],
        scratch_shapes=[pltpu.SMEM((owners,), jnp.int32), dma((owners, 2)), dma((cap, 2))],
        compiler_params=pltpu.CompilerParams(vmem_limit_bytes=VMEM_LIMIT),
        name="pack",
    )(block_request, block_index, handed_exponent, handed_latent, handed_rotary)

    got_latent, got_rotary, got_meta, tokens, token_rot, mixed = pl.pallas_call(
        functools.partial(exchange_kernel, owners, groups),
        out_shape=[shape((owners, groups, rows, width), bf16), shape((owners, groups, rot_rows, block_rows), bf16),
                   shape((owners, 1, LANES), jnp.int32), shape((steps * req_dev, width), bf16),
                   shape((steps * req_dev, query_rotary.shape[3]), bf16), shape((steps, req_dev, heads, width), bf16)],
        in_specs=[smem, vmem] + [hbm] * 9,
        out_specs=[vmem, vmem, vmem, vmem, vmem, hbm],
        scratch_shapes=[pltpu.VMEM((2, blocks, block_rows, width), bf16),
                        pltpu.VMEM((2, blocks, rot_width, block_rows), bf16),
                        pltpu.VMEM((2, steps, heads, width), bf16),
                        pltpu.VMEM((2, steps, heads, query_rotary.shape[3]), bf16),
                        pltpu.VMEM((2, steps, heads, width), bf16),
                        pltpu.VMEM((groups,) + token_latent.shape, bf16),
                        pltpu.VMEM((groups,) + token_rotary.shape, bf16),
                        dma((2, 4)), dma((2,)), dma((3,)), dma((owners, PIECES + 2)), dma((owners, PIECES + 2)),
                        dma((owners, across - 1, min(PIECES, rows // 16) + 1)), dma((owners, across - 1, min(PIECES, rows // 16) + 1)),
                        dma((owners, across, 2)), dma((owners, across, 2)),
                        dma((groups, 2)), dma((groups, 2))],
        compiler_params=pltpu.CompilerParams(collective_id=0, has_side_effects=True, vmem_limit_bytes=VMEM_LIMIT),
        name="exchange",
    )(lengths, cache_exponent, query_latent, query_rotary, cache_latent, cache_rotary, send_latent, send_rotary,
      send_meta, token_latent, token_rotary)

    mixed = pl.pallas_call(
        finish_kernel,
        out_shape=shape((steps, req_dev, heads, width), bf16),
        in_specs=[smem, smem, vmem, vmem] + [hbm] * 7,
        out_specs=hbm,
        input_output_aliases={10: 0},
        scratch_shapes=[pltpu.VMEM((hand, blocks, block_rows, width), bf16),
                        pltpu.VMEM((hand, blocks, rot_width, block_rows), bf16),
                        pltpu.VMEM((hand, steps, heads, width), bf16),
                        pltpu.VMEM((hand, steps, heads, query_rotary.shape[3]), bf16),
                        pltpu.VMEM((hand, steps, heads, width), bf16),
                        dma((owners, groups, 2)), dma((hand, 2)), dma((hand,))],
        compiler_params=pltpu.CompilerParams(vmem_limit_bytes=VMEM_LIMIT),
        name="finish",
    )(lengths, got_meta, tokens, token_rot, query_latent, query_rotary, own_latent, own_rotary, got_latent, got_rotary,
      mixed)

    output = jnp.einsum("srhc,hcv->srhv", mixed, value_up, preferred_element_type=f32).astype(bf16)
    return output.reshape(steps, req_dev, -1)


def solution(mesh):
    placed = (
        P(None, "dp", "tp", None),
        P(None, "dp", "tp", None),
        P(None, "dp", "tp"),
        P(None, "dp", "tp"),
        P("dp", None, None, None),
        P("dp", None, None, None),
        P("dp", None, None),
        P("dp", None, None),
        P("dp", None, None),
        P("dp", None),
        P("dp"),
        P("dp"),
        P("dp"),
        P("tp", None, None),
    )
    return jax.shard_map(
        local, mesh=mesh, in_specs=placed, out_specs=P(None, "dp", "tp"), check_vma=False
    )
```
